128 devices in a mesh: section: 2 (over x_lo), fsdp: 4 (over x_hi, core), tensor: 16 (over y, z).
Axes of the slice: x: 4 (x_hi: 2, x_lo: 2; x = x_hi * 2 + x_lo), y: 4, z: 4, core: 2. Of those that a mesh axis runs over, the one named last changes fastest.
Arguments:
- ends_in: bfloat16 [2, 4, 4, 1024, 1152], P('section', None, 'fsdp', 'tensor'), may hold values from -6 to 6
- w_qkv: bfloat16 [2, 1152, 3, 1152], P('section', 'fsdp', None, 'tensor'), may hold values from -0.1875 to 0.1875
- b_qv: float32 [2, 2, 1152], P('section', None, 'tensor'), may hold values from -0.6 to 0.6
- w_out: bfloat16 [2, 1152, 1152], P('section', 'tensor', 'fsdp'), may hold values from -1.5 to 1.5
- w_up: bfloat16 [2, 1152, 4304], P('section', 'fsdp', 'tensor'), may hold values from -0.1875 to 0.1875
- b_up: float32 [2, 4304], P('section', 'tensor'), may hold values from -3 to 3
- w_down: bfloat16 [2, 4304, 1152], P('section', 'tensor', 'fsdp'), may hold values from -0.09375 to 0.09375
- gains: float32 [2, 2, 1152], P('section', None, ('fsdp', 'tensor')), may hold values from 0.1 to 1.9
- shifts: float32 [2, 4, 1152], P('section', None, ('fsdp', 'tensor')), may hold values from -1.8 to 1.8
Outputs:
- ends_out: bfloat16 [2, 4, 4, 1024, 1152], P('section', None, 'fsdp', 'tensor')
- grad_w_qkv: float32 [2, 1152, 3, 1152], P('section', 'fsdp', None, 'tensor')
- grad_b_qv: float32 [2, 2, 1152], P('section', None, 'tensor')
- grad_w_out: float32 [2, 1152, 1152], P('section', 'tensor', 'fsdp')
- grad_w_up: float32 [2, 1152, 4304], P('section', 'fsdp', 'tensor')
- grad_b_up: float32 [2, 4304], P('section', 'tensor')
- grad_w_down: float32 [2, 4304, 1152], P('section', 'tensor', 'fsdp')
- grad_gains: float32 [2, 2, 1152], P('section', None, ('fsdp', 'tensor'))
- grad_shifts: float32 [2, 4, 1152], P('section', None, ('fsdp', 'tensor'))
The draws below stay inside these ranges and needn't reach their ends.
All inputs are finite; a program needn't handle non-finite values.
Results may differ from the reference program's by a relative error of at most 0.017.
Values may be sent and summed in bfloat16 or wider, within the bound.
No kernel may reach another device: no remote copies, remote signals or barrier semaphores. Data moves between devices by JAX's collectives and lax.ppermute only.
A program may use at most 256 MiB of HBM per device.

```python
import jax
import jax.numpy as jnp
from jax import lax

D = 1152
HEADS = 16
HD = 72
FF = 4304
SEQ = 1024
MICRO = 4
IMAGES = 4
SECTIONS = 2
N_SECTION = 2


def level_of(stream_key, shape, shards, smallest, high):
    def one(dim, blocks):
        heights = jax.random.uniform(jax.random.fold_in(jax.random.fold_in(stream_key, 6), dim), (blocks,), jnp.float32, smallest / len(shards), high / len(shards))
        return jnp.repeat(jnp.exp(heights), shape[dim] // blocks).reshape((-1,) + (1,) * (len(shape) - dim - 1))

    loudness = one(*shards[0])
    for cut in shards[1:]:
        loudness = loudness * one(*cut)
    return loudness


def noise(own_key, extent, scale, reach, pieces=(), dtype=jnp.bfloat16):
    loudness = level_of(own_key, extent, pieces, -0.22, 0.18) if pieces else 1.0
    result = jax.random.normal(own_key, extent, jnp.float32) * scale * loudness
    return jnp.minimum(jnp.maximum(result, -reach), reach).astype(dtype)


def setup_inputs(seed: int = 0) -> dict:
    keys = jax.random.split(jax.random.key(seed), 10)
    return {
        "ends_in": noise(keys[0], (SECTIONS, MICRO, IMAGES, SEQ, D), 1.0, 6.0, ((0, 2), (2, 4), (3, 16))),
        "w_qkv": noise(keys[1], (SECTIONS, D, 3, D), D ** -0.5, 0.1875, ((0, 2), (1, 4), (3, 16))),
        "b_qv": noise(keys[2], (SECTIONS, 2, D), 0.1, 0.6, ((0, 2), (2, 16)), jnp.float32),
        "w_out": noise(keys[3], (SECTIONS, D, D), (D // 64) ** -0.5, 1.5, ((0, 2), (1, 16), (2, 4))),
        "w_up": noise(keys[4], (SECTIONS, D, FF), D ** -0.5, 0.1875, ((0, 2), (1, 4), (2, 16))),
        "b_up": noise(keys[5], (SECTIONS, FF), 0.5, 3.0, ((0, 2), (1, 16)), jnp.float32),
        "w_down": noise(keys[6], (SECTIONS, FF, D), FF ** -0.5, 0.09375, ((0, 2), (1, 16), (2, 4))),
        "gains": jnp.clip(1.0 + 0.18 * jax.random.normal(keys[7], (SECTIONS, 2, D), jnp.float32), 0.1, 1.9),
        "shifts": noise(keys[8], (SECTIONS, 4, D), 0.3, 1.8, ((0, 2), (2, 64)), jnp.float32),
    }


@jax.custom_vjp
def low(v):
    return lax.optimization_barrier(v.astype(jnp.bfloat16)).astype(jnp.float32)

@jax.custom_vjp
def low_back(v):
    return v

def low_keep(v):
    return (low(v), None)

def low_pass(kept, grad):
    return (grad,)

def back_keep(v):
    return (v, None)

def back_low(kept, grad):
    return (low(grad),)
low.defvjp(low_keep, low_pass)
low_back.defvjp(back_keep, back_low)
norm_epsilon = 1e-06
highest = lax.Precision.HIGHEST

def norm_rows(hidden, gain_row, offset_row):
    average = lax.optimization_barrier(jnp.mean(hidden, axis=-1, keepdims=True))
    centered = hidden - average
    inv_spread = lax.rsqrt(lax.optimization_barrier(jnp.mean(centered * centered, axis=-1, keepdims=True)) + norm_epsilon)
    return centered * inv_spread * gain_row + offset_row

def attend(triple):
    query_rows, key_rows, value_rows = triple
    raw_scores = jnp.einsum('qhe,khe->hqk', query_rows, key_rows, precision=highest) * HD ** (-0.5)
    scores = low_back(raw_scores)
    attention = low(jax.nn.softmax(scores, axis=-1))
    mixed_heads = jnp.einsum('hqk,khe->qhe', attention, value_rows, precision=highest)
    return low_back(low(mixed_heads))

def split_heads(merged):
    return merged.reshape(merged.shape[0], SEQ, HEADS, HD)

def encoder_layer(hidden, w_qkv, b_qv, w_out, w_up, b_up, w_down, gains, shifts):
    count_images = hidden.shape[0]
    normed_first = low(norm_rows(hidden, gains[0], shifts[0]))
    projected = jnp.einsum('nsd,dcf->cnsf', normed_first, w_qkv, precision=highest)
    query_rows = low(low_back(projected[0]) + b_qv[0])
    key_rows = low(low_back(projected[1]))
    value_rows = low(low_back(projected[2]) + b_qv[1])
    mixed = lax.map(jax.checkpoint(attend), (split_heads(query_rows), split_heads(key_rows), split_heads(value_rows)))
    mixed = mixed.reshape(count_images, SEQ, D)
    middle = hidden + low_back(jnp.einsum('nsf,fd->nsd', mixed, w_out, precision=highest)) + shifts[1]
    normed_second = low(norm_rows(middle, gains[1], shifts[2]))
    pre_act = low_back(jnp.einsum('nsd,df->nsf', normed_second, w_up, precision=highest)) + b_up
    activated = low(jax.nn.gelu(pre_act, approximate=True))
    return middle + low_back(jnp.einsum('nsf,fd->nsd', activated, w_down, precision=highest)) + shifts[3]

def reference(ends_in, w_qkv, b_qv, w_out, w_up, b_up, w_down, gains, shifts):
    count_images = MICRO * IMAGES
    inputs = ends_in[0].astype(jnp.float32).reshape(count_images, SEQ, D)
    cotangent = ends_in[1].astype(jnp.float32).reshape(count_images, SEQ, D)
    parameters = tuple((item.astype(jnp.float32) for item in (w_qkv, b_qv, w_out, w_up, b_up, w_down, gains, shifts)))

    def network(start, *weights):
        hidden = start
        for section_index in range(N_SECTION):
            if section_index > 0:
                hidden = low_back(low(hidden))
            hidden = encoder_layer(hidden, *[item[section_index] for item in weights])
        return hidden
    output, pullback = jax.vjp(network, inputs, *parameters)
    gradients = pullback(cotangent)
    ends_out = jnp.stack([gradients[0].reshape(MICRO, IMAGES, SEQ, D), output.reshape(MICRO, IMAGES, SEQ, D)]).astype(jnp.bfloat16)
    return (ends_out, gradients[1], gradients[2], gradients[3], gradients[4], gradients[5], gradients[6], gradients[7], gradients[8])
```

```python
import functools

import jax
import jax.numpy as jnp
from jax import lax
from jax.experimental import pallas as pl
from jax.experimental.pallas import tpu as pltpu
from jax.sharding import Mesh
from jax.sharding import PartitionSpec as P

AXES = ("xl", "xh", "c", "y", "z")
EPSILON = 1e-06
BF = jnp.bfloat16
F32 = jnp.float32
LANES = 128
CHEAP = pl.CostEstimate(flops=1 << 20, bytes_accessed=1 << 16, transcendentals=0)


def swap(value, axis):
    return lax.ppermute(value, axis, [(0, 1), (1, 0)])


def pick(flag, if_true, if_false):
    return jnp.where(flag, if_true, if_false)


def dot(spec, left, right):
    return jnp.einsum(spec, left, right, preferred_element_type=F32)


def norm_rows(hidden, gain_row, offset_row):
    average = jnp.mean(hidden, axis=-1, keepdims=True)
    centered = hidden - average
    inv_spread = lax.rsqrt(jnp.mean(centered * centered, axis=-1, keepdims=True) + EPSILON)
    normed = centered * inv_spread
    return (normed * gain_row + offset_row).astype(BF), normed, inv_spread


def norm_back(carried, grad_normed, normed, inv_spread, gain_row):
    scaled = grad_normed * gain_row
    inner_mean = jnp.mean(scaled, axis=-1, keepdims=True)
    cross_mean = jnp.mean(scaled * normed, axis=-1, keepdims=True)
    grad_hidden = carried + inv_spread * (scaled - inner_mean - normed * cross_mean)
    return grad_hidden, jnp.sum(grad_normed * normed, axis=0), jnp.sum(grad_normed, axis=0)


def gelu_tanh(values):
    return jax.nn.gelu(values, approximate=True)


def product(left, right, left_dim, right_dim):
    return lax.dot_general(left, right, (((left_dim,), (right_dim,)), ((), ())), preferred_element_type=F32)


def probabilities(query, keys, scale):
    scores = [product(key, query, 1, 1) * scale for key in keys]
    top = jnp.maximum(*(jnp.max(block, axis=0, keepdims=True) for block in scores))
    raised = [jnp.exp(block - top) for block in scores]
    weight = 1.0 / sum(jnp.sum(block, axis=0, keepdims=True) for block in raised)
    return [block * weight for block in raised]


def head(ref, index):
    return ref[:, index * LANES : (index + 1) * LANES]


def attend_kernel(scale, query, own, other, out):
    for h in range(4):
        probs = probabilities(head(query, h), (head(own, h), head(other, h)), scale)
        mixed = product(head(own, 4 + h), probs[0].astype(BF), 0, 0)
        mixed += product(head(other, 4 + h), probs[1].astype(BF), 0, 0)
        out[:, h * LANES : (h + 1) * LANES] = mixed.T.astype(BF)


def attend_back_kernel(scale, query, own, other, grad, grad_query, sum_query, grad_own, grad_other):
    for h in range(4):
        place = slice(h * LANES, (h + 1) * LANES)
        rows, pull = head(query, h), head(grad, h)
        keys = head(own, h), head(other, h)
        probs = probabilities(rows, keys, scale)
        pulled = [product(head(ref, 4 + h), pull, 1, 1) for ref in (own, other)]
        mean = sum(jnp.sum(p * g, axis=0, keepdims=True) for p, g in zip(probs, pulled))
        scores = [(p * (g - mean)).astype(BF) for p, g in zip(probs, pulled)]
        turned = sum(product(key, block, 0, 0) for key, block in zip(keys, scores))
        from_query = turned.T * scale
        grad_query[:, place] = from_query.astype(BF)
        sum_query[:, place] = jnp.sum(from_query, axis=0, keepdims=True)
        for result, p, s in zip((grad_own, grad_other), probs, scores):
            result[0, :, place] = (product(s, rows, 1, 0) * scale).astype(result.dtype)
            result[1, :, place] = product(p.astype(BF), pull, 1, 0).astype(result.dtype)


def on_vmem(kernel, out_shape, limit, *args, flags=0):
    vmem = pl.BlockSpec(memory_space=pltpu.VMEM)
    return pl.pallas_call(
        kernel,
        in_specs=[pl.BlockSpec(memory_space=pltpu.SMEM)] * flags + [vmem] * (len(args) - flags),
        out_specs=jax.tree.map(lambda _: vmem, out_shape),
        out_shape=out_shape,
        compiler_params=pltpu.CompilerParams(vmem_limit_bytes=limit << 20),
        cost_estimate=CHEAP,
    )(*args)


def attend(query, own, other, hd):
    out = jax.ShapeDtypeStruct(query.shape, BF)
    return on_vmem(functools.partial(attend_kernel, hd**-0.5), out, 24, query, own, other)


def attend_back(query, own, other, grad, hd):
    rows, width = query.shape
    out = [
        jax.ShapeDtypeStruct((rows, width), BF),
        jax.ShapeDtypeStruct((1, width), F32),
        jax.ShapeDtypeStruct((2, rows, width), F32),
        jax.ShapeDtypeStruct((2, rows, width), BF),
    ]
    return on_vmem(functools.partial(attend_back_kernel, hd**-0.5), out, 24, query, own, other, grad)


def outer_kernel(with_sum, tile, flag, left_one, right_one, left_two, right_two, *rest):
    out = rest[-1]

    def result(left, right):
        def step(index, carry):
            place = pl.ds(pl.multiple_of(index * tile, LANES), tile)
            total = product(left[...], right[:, place], 0, 0)
            if with_sum:
                total += rest[0][:, place].astype(F32)
            out[:, place] = total.astype(out.dtype)
            return carry

        lax.fori_loop(0, out.shape[1] // tile, step, 0)

    @pl.when(flag[0] == 1)
    def _():
        result(left_one, right_one)

    @pl.when(flag[0] != 1)
    def _():
        result(left_two, right_two)


def outer(flag, one, two, summand=None):
    units, width = one[0].shape[1], one[1].shape[1]
    tile = width // 3 if width % 384 == 0 else width
    extra = [] if summand is None else [summand]
    kernel = functools.partial(outer_kernel, bool(extra), tile)
    out = jax.ShapeDtypeStruct((units, width), BF)
    return on_vmem(kernel, out, 24, flag, *one, *two, *extra, flags=1)


def cut_kernel(first, second, out):
    quarter = out.shape[2]
    for layer, part in enumerate((first, second)):
        for i in range(4):
            out[layer * 4 + i] = part[:, i * quarter : (i + 1) * quarter].astype(BF)


def owned_mask(piece, devices, width):
    column = lax.broadcasted_iota(jnp.int32, (devices, width), 1)
    start = lax.broadcasted_iota(jnp.int32, (devices, width), 0) * piece
    return jnp.logical_and(column >= start, column < start + piece)


def exact(left, chosen):
    high = left.astype(BF)
    rest = left - high.astype(F32)
    middle = rest.astype(BF)
    low = (rest - middle.astype(F32)).astype(BF)
    return sum(product(part, chosen, 1, 0) for part in (low, middle, high))


def unpack_kernel(piece, phase, table, out):
    devices, width = table.shape[0] // 2, phase.shape[1]
    mask = owned_mask(piece, devices, width)
    lane = lax.broadcasted_iota(jnp.int32, (LANES, width), 0)
    for vector in range(out.shape[0]):
        spread = exact(table[...], (lane - vector * piece == phase[...]).astype(BF))
        for layer in range(2):
            rows = spread[layer * devices : (layer + 1) * devices]
            out[vector, layer : layer + 1] = jnp.sum(jnp.where(mask, rows, 0.0), axis=0, keepdims=True)


def pack_kernel(piece, phase, grads, out):
    devices, width = out.shape[1], phase.shape[0]
    mask = owned_mask(piece, devices, width)
    lane = lax.broadcasted_iota(jnp.int32, (width, LANES), 1)
    for layer in range(2):
        total = jnp.zeros((devices, LANES), F32)
        for vector in range(grads.shape[0]):
            rows = jnp.broadcast_to(grads[vector, layer : layer + 1], (devices, width))
            total += exact(jnp.where(mask, rows, 0.0), (lane - vector * piece == phase[...]).astype(BF))
        out[layer] = total


def unpack_vectors(table, width):
    piece = width // 64
    phase = (jnp.arange(width, dtype=jnp.int32) % piece)[None]
    out = jax.ShapeDtypeStruct((6, 2, width), F32)
    return on_vmem(functools.partial(unpack_kernel, piece), out, 16, phase, table)


def pack_vectors(grads):
    width = grads.shape[2]
    piece = width // 64
    phase = (jnp.arange(width, dtype=jnp.int32) % piece)[:, None]
    out = jax.ShapeDtypeStruct((2, 64, LANES), F32)
    return on_vmem(functools.partial(pack_kernel, piece), out, 16, phase, grads)


def tie(*values):
    return lax.optimization_barrier(values)


def ring(value, axis, step):
    return lax.ppermute(value, axis, [(i, (i + step) % 4) for i in range(4)])


def spread_near(rows):
    return ring(rows, "z", 1), ring(rows, "z", -1)


def spread_far(near):
    below, above = near
    half = below.shape[0] // 2
    return ring(below[:half], "z", 1), ring(above[half:], "z", -1)


def join(rows, near, far):
    return jnp.concatenate([rows, *near, *far], axis=0)


def chunks_of(summand):
    count = summand.shape[0] // 4
    low = summand.astype(BF)
    return [low[i * count : (i + 1) * count] for i in range(4)]


def collect_far(chunks, axis="z"):
    far = chunks[3]
    half = far.shape[0] // 2
    return ring(far[:half], axis, 1), ring(far[half:], axis, -1)


def collect_near(chunks, passed, axis="z"):
    own, below, above, _ = chunks
    half = own.shape[0] // 2
    above_one = (above[:half].astype(F32) + passed[0].astype(F32)).astype(BF)
    below_two = (below[half:].astype(F32) + passed[1].astype(F32)).astype(BF)
    from_below = ring(jnp.concatenate([above_one, above[half:]], axis=0), axis, 1)
    from_above = ring(jnp.concatenate([below[:half], below_two], axis=0), axis, -1)
    return own.astype(F32) + from_below.astype(F32) + from_above.astype(F32)


def pad_heads(rows, hd):
    return jnp.pad(rows, ((0, 0), (0, LANES - hd), (0, 0))).reshape(4 * LANES, rows.shape[2])


def attn_weights(own, other, on_first):
    first, second = pick(on_first, own, other), pick(on_first, other, own)
    hd = own.shape[1] // 2
    w_query = pad_heads(first[:, :hd], hd)
    w_pair = jnp.concatenate([pad_heads(first[:, hd:], hd), pad_heads(second[:, :hd], hd)])
    return w_query, w_pair, pad_heads(second[:, hd:], hd)


def mlp_weights(own, other, on_first):
    shape = (-1, own.shape[2])
    return pick(on_first, own, other).reshape(shape), pick(on_first, other, own).reshape(shape)


def from_owners(part):
    rows, quarter = part.shape[1:]
    sent = jnp.broadcast_to(part[None], (4, 2, rows, quarter)).reshape(8, rows, quarter)
    arrived = lax.all_to_all(sent, ("xl", "xh", "c"), 0, 0).reshape(2, 4, rows, quarter)
    return [jnp.concatenate([arrived[layer, i] for i in range(4)], axis=-1) for layer in range(2)]


def to_owners(parts):
    rows, width = parts[0].shape
    out = jax.ShapeDtypeStruct((8, rows, width // 4), BF)
    chunks = on_vmem(cut_kernel, out, 16, *parts)
    arrived = lax.all_to_all(chunks, ("xl", "xh", "c"), 0, 0)
    return jnp.sum(arrived.reshape(4, 2, rows, width // 4).astype(F32), axis=0)


def by_xor(values, index):
    odd, high = index % 2 == 1, index >= 2
    values = [pick(odd, values[i ^ 1], values[i]) for i in range(4)]
    return [pick(high, values[i ^ 2], values[i]) for i in range(4)]


def token_routes():
    routes = []
    for step in range(4):
        route = []
        for a in range(2):
            for b in range(2):
                for y in range(4):
                    m = (2 * a + y % 2) ^ step
                    route.append(((a * 2 + b) * 4 + y, (b * 2 + y // 2) * 4 + m))
        routes.append(route)
    return routes


def x_ring():
    order = [xl_at * 2 + xh_at for xh_at in range(2) for xl_at in range(2)]
    up = [(order[i], order[(i + 1) % 4]) for i in range(4)]
    return up, [(b, a) for a, b in up]


def from_owners_ring(part, on_first):
    kept, given = pick(on_first, part[0], part[1]), pick(on_first, part[1], part[0])
    got = swap(given, "c")
    block = jnp.concatenate([pick(on_first, kept, got), pick(on_first, got, kept)], axis=-1)
    half = block.shape[0] // 2
    up, down = x_ring()
    below, above = lax.ppermute(block, ("xl", "xh"), up), lax.ppermute(block, ("xl", "xh"), down)
    far = jnp.concatenate(
        [lax.ppermute(below[:half], ("xl", "xh"), up), lax.ppermute(above[half:], ("xl", "xh"), down)]
    )
    turn = 2 * lax.axis_index("xh") + lax.axis_index("xl")

    def source(x):
        away = (x - turn) % 4
        return pick(away == 0, block, pick(away == 1, above, pick(away == 2, far, below)))

    return [jnp.concatenate([source(layer), source(layer + 2)], axis=-1) for layer in range(2)]


def forward_layer(hidden, rows1, attn_own, mlp_own, vectors, b_query, b_pair, b_up, hd, on_first, attn_other, late, beside):
    w_query, w_pair, w_out = attn_weights(attn_own, attn_other, on_first)
    own = (dot("nd,fd->nf", rows1, w_pair) + b_pair).astype(BF)
    other = swap(own, "c")
    query = (dot("nd,fd->nf", rows1, w_query) + b_query).astype(BF)
    attn = attend(query, own, other, hd)
    attn, beside = tie(attn, beside)
    chunks = chunks_of(dot("nf,fd->nd", attn, w_out))
    passed, mlp_own = tie(collect_far(chunks), mlp_own)
    branch, mlp_other = tie(collect_near(chunks, passed), swap(mlp_own, "c"))
    middle = hidden + (branch + vectors[3])
    a2, unit2, rstd2 = norm_rows(middle, vectors[1], vectors[4])
    near, (w_up, w_down) = tie(spread_near(a2), mlp_weights(mlp_own, mlp_other, on_first))
    rows2 = join(a2, near, spread_far(near))
    pre = dot("nd,kd->nk", rows2, w_up) + b_up
    act = gelu_tanh(pre).astype(BF)
    stored = (rows1, query, own, other, attn, unit2, rstd2, rows2, pre, act)
    weights = (w_query, w_pair, w_out, w_up, w_down)
    if late is None:
        return middle, stored, weights, beside
    chunks = chunks_of(dot("nk,kd->nd", act, w_down))
    summed, held = tie(collect_near(chunks, collect_far(chunks)), late(mlp_own))
    result = middle + (summed + vectors[5])
    return result, stored, weights, held, beside


def backward_layer(grad_out, down_rows, stored, unit_rows, unit1, rstd1, weights, vectors, on_first, hd, beside, to_owner):
    rows1, query, own, other, attn, unit2, rstd2, rows2, pre, act = stored
    w_query, w_pair, w_out, w_up, w_down = weights
    grad_act = dot("nd,kd->nk", down_rows, w_down)
    grad_pre = jax.vjp(gelu_tanh, pre)[1](grad_act)[0]
    pre_low = grad_pre.astype(BF)
    summand = dot("nk,kd->nd", pre_low, w_up).astype(BF)
    if beside is not None:
        beside = chunks_of(dot("nk,kd->nd", beside, w_down))
        summand, pre_low, beside_passed = tie(summand, pre_low, collect_far(beside))
    else:
        summand, pre_low = tie(summand, pre_low)
    chunks = chunks_of(summand)
    up_pair, down_pair = (pre_low, rows2), (act, down_rows)
    flag = on_first.astype(jnp.int32).reshape(1)
    ga2, given = tie(collect_near(chunks, collect_far(chunks)), outer(flag, down_pair, up_pair))
    grad_middle, gain2, offset2 = norm_back(grad_out, ga2, unit2, rstd2, vectors[1])
    go = grad_middle.astype(BF)
    near, part_mlp = tie(spread_near(go), outer(flag, up_pair, down_pair, swap(given, "c")))
    part_mlp = lax.psum_scatter(part_mlp.reshape(4, -1, part_mlp.shape[1]), "y", scatter_dimension=0, tiled=False)
    far = spread_far(near)
    if beside is not None:
        far, beside_passed = tie(far, beside_passed)
    out_rows = join(go, near, far)
    gattn = dot("nd,fd->nf", out_rows, w_out).astype(BF)
    grad_query, sum_query, grad_own, grad_other = attend_back(query, own, other, gattn, hd)
    if beside is not None:
        grad_other, beside = tie(grad_other, collect_near(beside, beside_passed))
    sent = swap(grad_other, "c")
    grad_w_out = dot("nf,nd->fd", attn, out_rows).astype(BF)
    grad_w_query = dot("nf,nd->fd", grad_query, rows1).astype(BF)
    from_query = dot("nf,fd->nd", grad_query, w_query)
    sent, part_mlp, grad_w_out, grad_w_query, from_query = tie(sent, part_mlp, grad_w_out, grad_w_query, from_query)
    pair = grad_own + sent.astype(F32)
    sum_value = jnp.sum(pair[1], axis=0)
    pair = pair.astype(BF)
    partial = from_query + dot("nf,fd->nd", jnp.concatenate([pair[0], pair[1]], axis=1), w_pair)
    gain1, offset1 = jnp.sum(partial * unit_rows, axis=0), jnp.sum(partial, axis=0)
    chunks = chunks_of(partial)

    def heads(rows):
        return rows.reshape(4, LANES, -1)[:, :hd]

    def attn_grads(pair):
        grad_w_key, grad_w_value = (dot("nf,nd->fd", pair[i], rows1).astype(BF) for i in range(2))
        first = jnp.concatenate([heads(grad_w_query), heads(grad_w_key)], axis=1)
        second = jnp.concatenate([heads(grad_w_value), heads(grad_w_out)], axis=1)
        return pick(on_first, second, first), pick(on_first, first, second)

    passed, pair, part_mlp = tie(collect_far(chunks), pair, part_mlp)
    given, kept = attn_grads(pair)
    part_mlp = to_owner(part_mlp)
    part_attn = (kept.astype(F32) + swap(given, "c").astype(F32)).astype(BF)
    ga1, gain1, offset1 = tie(collect_near(chunks, passed), gain1, offset1)
    grad_hidden = norm_back(grad_middle, ga1, unit1, rstd1, vectors[0])[0]
    grad_vectors = [gain1, gain2, offset1, jnp.sum(grad_middle, axis=0), offset2, jnp.sum(grad_out, axis=0)]
    grad_b_up = jnp.sum(grad_pre, axis=0)
    grad_b_qv = jnp.stack([sum_query[0], sum_value]).reshape(2, 4, LANES)
    return grad_hidden, part_attn, part_mlp, (grad_vectors, grad_b_qv, grad_b_up), beside


def body(ends_in, w_qkv, b_qv, w_out, w_up, b_up, w_down, gains, shifts):
    xl, core, own_y, own_z = (lax.axis_index(axis) for axis in ("xl", "c", "y", "z"))
    local = ends_in[0, :, 0]
    _, rows, width = local.shape
    hd = w_qkv.shape[3]
    units = w_up.shape[2]
    padded = -(-units // 16) * 16
    spare = padded - units

    on_first = core == 0
    qkv_rows = jnp.transpose(w_qkv[0], (1, 2, 0))
    pad_rows = ((0, spare), (0, 0))
    attn_rows = jnp.stack([qkv_rows[:2].reshape(2 * hd, -1), jnp.concatenate([qkv_rows[2], w_out[0]], axis=0)])
    mlp_rows = jnp.stack([jnp.pad(w_up[0].T, pad_rows), jnp.pad(w_down[0], pad_rows)])
    attn_rows, local = tie(attn_rows, local)
    attn_parts = from_owners(attn_rows)

    place = 2 * xl + own_y % 2
    routes = token_routes()
    blocks = by_xor([local[m] for m in range(4)], place)
    blocks = [lax.ppermute(block, ("xl", "c", "y"), route) for block, route in zip(blocks, routes)]
    blocks = by_xor(blocks, own_y)
    start_low, cot_low = jnp.concatenate(blocks[:2]), jnp.concatenate(blocks[2:])
    piece = width // 64
    up_lines = -(-padded // LANES)
    lines = -(-(3 + up_lines) // 8) * 8

    def line(values, count):
        return jnp.pad(values, (0, count * LANES - values.shape[0])).reshape(count, LANES)

    own = [line(jnp.concatenate([gains[0].ravel(), shifts[0].ravel()]), 1), line(b_qv[0, 0], 1), line(b_qv[0, 1], 1)]
    own = jnp.concatenate(own + [line(b_up[0], lines - 3)])[None]
    near = spread_near(start_low)
    own, attn0_part, mlp_rows = tie(own, attn_parts[0], mlp_rows)
    attn0_own = lax.all_gather(attn0_part, "y", axis=0)
    table = lax.all_to_all(jnp.broadcast_to(own, (128, lines, LANES)), AXES, 0, 0)
    start_rows = join(start_low, near, spread_far(near))
    mlp_parts = from_owners_ring(mlp_rows, on_first)
    attn0_own, mlp_parts, attn1_part = tie(attn0_own, mlp_parts, attn_parts[1])
    mlp0_own = lax.all_gather(mlp_parts[0], "y", axis=0)
    part1 = jnp.concatenate([attn1_part, mlp_parts[1]])

    vectors = jnp.swapaxes(unpack_vectors(table[:, 0], width), 0, 1)
    biases = lax.dynamic_index_in_dim(table.reshape(2, 4, 4, 4, lines, LANES)[:, 0], own_z, 2, keepdims=False)
    bias_qv = biases[:, :, 1:3].transpose(0, 2, 1, 3)
    bias_up = biases[:, :, 3 : 3 + up_lines].reshape(2, 4, -1)[..., :padded].reshape(2, -1)
    bias_qv = bias_qv.reshape(2, 2, 4 * LANES)
    bias_pair = jnp.concatenate([jnp.zeros_like(bias_qv[:, 1]), bias_qv[:, 1]], axis=-1)

    start, cotangent = start_low.astype(F32), cot_low.astype(F32)
    rows0, unit_rows0, _ = norm_rows(start_rows.astype(F32), vectors[0, 0], vectors[0, 2])
    _, unit0, rstd0 = norm_rows(start, vectors[0, 0], vectors[0, 2])
    def fetch_next(after):
        own = tie(after, part1)[1]
        return lax.all_gather(own, "y", axis=0)

    middle, stored0, weights0, own1, cot_near = forward_layer(
        start, rows0, attn0_own, mlp0_own, vectors[0], bias_qv[0, 0], bias_pair[0], bias_up[0], hd, on_first,
        swap(attn0_own, "c"), fetch_next, spread_near(cot_low),
    )
    attn1_own, mlp1_own = own1[:, : 2 * hd], own1[:, 2 * hd :]
    middle = middle.astype(BF)
    near, attn1_own, attn1_other = tie(spread_near(middle), attn1_own, swap(attn1_own, "c"))
    middle_rows = join(middle, near, spread_far(near)).astype(F32)
    middle = middle.astype(F32)
    rows1, unit_rows1, _ = norm_rows(middle_rows, vectors[1, 0], vectors[1, 2])
    _, unit1, rstd1 = norm_rows(middle, vectors[1, 0], vectors[1, 2])
    middle1, stored1, weights1, cot_far = forward_layer(
        middle, rows1, attn1_own, mlp1_own, vectors[1], bias_qv[1, 0], bias_pair[1], bias_up[1], hd, on_first,
        attn1_other, None, spread_far(cot_near),
    )
    down_rows = join(cot_low, cot_near, cot_far)
    grad1, attn1, mlp1, small1, branch = backward_layer(
        cotangent, down_rows, stored1, unit_rows1, unit1, rstd1, weights1, vectors[1], on_first, hd,
        stored1[-1], lambda part: part,
    )
    result = middle1 + (branch + vectors[1, 5])
    grad1 = grad1.astype(BF)
    near, attn1 = tie(spread_near(grad1), attn1)
    attn1 = lax.psum_scatter(attn1, "y", scatter_dimension=0, tiled=False)
    down_rows = join(grad1, near, spread_far(near))
    grad0, attn0, grad_mlp, small0, _ = backward_layer(
        grad1.astype(F32), down_rows, stored0, unit_rows0, unit0, rstd0, weights0, vectors[0], on_first, hd, None,
        lambda part: to_owners((part, mlp1)),
    )
    gvec1, gqv1, gup1 = small1
    gvec0, gqv0, gup0 = small0

    chunks = [lax.dynamic_index_in_dim(attn0, (own_y + step) % 4, 0, keepdims=False) for step in (0, 3, 1, 2)]
    half = rows
    out_grad, out_result = grad0.astype(BF), result.astype(BF)
    blocks = by_xor([out_grad[:half], out_grad[half:], out_result[:half], out_result[half:]], own_y)
    passed, blocks = tie(collect_far(chunks, "y"), blocks)
    attn0 = collect_near(chunks, passed, "y")
    blocks = [
        lax.ppermute(block, ("xl", "c", "y"), [(b, a) for a, b in route]) for block, route in zip(blocks, routes)
    ]
    ends_out = jnp.stack(by_xor(blocks, place))

    grad_vectors = jnp.stack(gvec0 + gvec1).reshape(2, 6, width).swapaxes(0, 1)
    grad_qv = jnp.stack([gqv0, gqv1]).transpose(0, 2, 1, 3)
    grad_up = jnp.stack([gup0, gup1]).reshape(2, 4, padded)
    grad_up = jnp.pad(grad_up, ((0, 0), (0, 0), (0, (lines - 3) * LANES - padded)))
    grad_bias = jnp.concatenate([grad_qv, grad_up.reshape(2, 4, lines - 3, LANES)], axis=2)
    here = (jnp.arange(4) == own_z)[:, None, None]
    grad_bias = jnp.where(here, grad_bias[:, None, :, None], 0.0)
    grad_bias = jnp.broadcast_to(grad_bias, (2, 4, 4, 4, lines - 1, LANES)).reshape(128, lines - 1, LANES)
    sent = jnp.concatenate([pack_vectors(grad_vectors).reshape(128, 1, LANES), grad_bias], axis=1)
    owned = lax.all_to_all(sent, AXES, 0, 0)

    grad_attn = to_owners((attn0, attn1))
    owned = jnp.sum(owned, axis=0)
    share_vec = owned[0, : 6 * piece].reshape(6, piece)
    share_qv = owned[1:3, :hd]
    share_b_up = owned[3:].reshape(-1)[:units]
    share_up = grad_mlp[0, :units].T
    share_down = grad_mlp[1, :units]
    heads = grad_attn.reshape(4, hd, -1)
    share_qkv = jnp.transpose(heads[:3], (2, 0, 1))
    share_out = heads[3]

    return (
        ends_out[None, :, None],
        share_qkv[None],
        share_qv[None],
        share_out[None],
        share_up[None],
        share_b_up[None],
        share_down[None],
        share_vec[None, :2],
        share_vec[None, 2:],
    )


def solution(mesh):
    fine = Mesh(mesh.devices.reshape(2, 2, 2, 4, 4), AXES)
    f, t = ("xh", "c"), ("y", "z")
    specs = (
        P("xl", None, f, t, None),
        P("xl", f, None, t),
        P("xl", None, t),
        P("xl", t, f),
        P("xl", f, t),
        P("xl", t),
        P("xl", t, f),
        P("xl", None, f + t),
        P("xl", None, f + t),
    )
    return jax.shard_map(body, mesh=fine, in_specs=specs, out_specs=specs, check_vma=False)
```

```python
import functools

import jax
import jax.numpy as jnp
from jax import lax
from jax.experimental import pallas as pl
from jax.experimental.pallas import tpu as pltpu
from jax.sharding import Mesh
from jax.sharding import PartitionSpec as P

AXES = ("xl", "xh", "c", "y", "z")
EPSILON = 1e-06
BF = jnp.bfloat16
F32 = jnp.float32
LANES = 128
CHEAP = pl.CostEstimate(flops=1 << 20, bytes_accessed=1 << 16, transcendentals=0)


def swap(value, axis):
    return lax.ppermute(value, axis, [(0, 1), (1, 0)])


def pick(flag, if_true, if_false):
    return jnp.where(flag, if_true, if_false)


def dot(spec, left, right):
    return jnp.einsum(spec, left, right, preferred_element_type=F32)


def norm_rows(hidden, gain_row, offset_row):
    average = jnp.mean(hidden, axis=-1, keepdims=True)
    centered = hidden - average
    inv_spread = lax.rsqrt(jnp.mean(centered * centered, axis=-1, keepdims=True) + EPSILON)
    normed = centered * inv_spread
    return (normed * gain_row + offset_row).astype(BF), normed, inv_spread


def norm_back(carried, grad_normed, normed, inv_spread, gain_row):
    scaled = grad_normed * gain_row
    inner_mean = jnp.mean(scaled, axis=-1, keepdims=True)
    cross_mean = jnp.mean(scaled * normed, axis=-1, keepdims=True)
    grad_hidden = carried + inv_spread * (scaled - inner_mean - normed * cross_mean)
    return grad_hidden, jnp.sum(grad_normed * normed, axis=0), jnp.sum(grad_normed, axis=0)


def gelu_tanh(values):
    return jax.nn.gelu(values, approximate=True)


def product(left, right, left_dim, right_dim):
    return lax.dot_general(left, right, (((left_dim,), (right_dim,)), ((), ())), preferred_element_type=F32)


def probabilities(query, keys, scale):
    scores = [product(key, query, 1, 1) * scale for key in keys]
    top = jnp.maximum(*(jnp.max(block, axis=0, keepdims=True) for block in scores))
    raised = [jnp.exp(block - top) for block in scores]
    weight = 1.0 / sum(jnp.sum(block, axis=0, keepdims=True) for block in raised)
    return [block * weight for block in raised]


def head(ref, index):
    return ref[:, index * LANES : (index + 1) * LANES]


def attend_kernel(scale, query, own, other, out):
    for h in range(4):
        probs = probabilities(head(query, h), (head(own, h), head(other, h)), scale)
        mixed = product(head(own, 4 + h), probs[0].astype(BF), 0, 0)
        mixed += product(head(other, 4 + h), probs[1].astype(BF), 0, 0)
        out[:, h * LANES : (h + 1) * LANES] = mixed.T.astype(BF)


def attend_back_kernel(scale, query, own, other, grad, grad_query, sum_query, grad_own, grad_other):
    for h in range(4):
        place = slice(h * LANES, (h + 1) * LANES)
        rows, pull = head(query, h), head(grad, h)
        keys = head(own, h), head(other, h)
        probs = probabilities(rows, keys, scale)
        pulled = [product(head(ref, 4 + h), pull, 1, 1) for ref in (own, other)]
        mean = sum(jnp.sum(p * g, axis=0, keepdims=True) for p, g in zip(probs, pulled))
        scores = [(p * (g - mean)).astype(BF) for p, g in zip(probs, pulled)]
        turned = sum(product(key, block, 0, 0) for key, block in zip(keys, scores))
        from_query = turned.T * scale
        grad_query[:, place] = from_query.astype(BF)
        sum_query[:, place] = jnp.sum(from_query, axis=0, keepdims=True)
        for result, p, s in zip((grad_own, grad_other), probs, scores):
            result[0, :, place] = (product(s, rows, 1, 0) * scale).astype(result.dtype)
            result[1, :, place] = product(p.astype(BF), pull, 1, 0).astype(result.dtype)


def on_vmem(kernel, out_shape, limit, *args, flags=0):
    vmem = pl.BlockSpec(memory_space=pltpu.VMEM)
    return pl.pallas_call(
        kernel,
        in_specs=[pl.BlockSpec(memory_space=pltpu.SMEM)] * flags + [vmem] * (len(args) - flags),
        out_specs=jax.tree.map(lambda _: vmem, out_shape),
        out_shape=out_shape,
        compiler_params=pltpu.CompilerParams(vmem_limit_bytes=limit << 20),
        cost_estimate=CHEAP,
    )(*args)


def attend(query, own, other, hd):
    out = jax.ShapeDtypeStruct(query.shape, BF)
    return on_vmem(functools.partial(attend_kernel, hd**-0.5), out, 24, query, own, other)


def attend_back(query, own, other, grad, hd):
    rows, width = query.shape
    out = [
        jax.ShapeDtypeStruct((rows, width), BF),
        jax.ShapeDtypeStruct((1, width), F32),
        jax.ShapeDtypeStruct((2, rows, width), F32),
        jax.ShapeDtypeStruct((2, rows, width), BF),
    ]
    return on_vmem(functools.partial(attend_back_kernel, hd**-0.5), out, 24, query, own, other, grad)


def outer_kernel(with_sum, tile, flag, left_one, right_one, left_two, right_two, *rest):
    out = rest[-1]

    def result(left, right):
        def step(index, carry):
            place = pl.ds(pl.multiple_of(index * tile, LANES), tile)
            total = product(left[...], right[:, place], 0, 0)
            if with_sum:
                total += rest[0][:, place].astype(F32)
            out[:, place] = total.astype(out.dtype)
            return carry

        lax.fori_loop(0, out.shape[1] // tile, step, 0)

    @pl.when(flag[0] == 1)
    def _():
        result(left_one, right_one)

    @pl.when(flag[0] != 1)
    def _():
        result(left_two, right_two)


def outer(flag, one, two, summand=None):
    units, width = one[0].shape[1], one[1].shape[1]
    tile = width // 3 if width % 384 == 0 else width
    extra = [] if summand is None else [summand]
    kernel = functools.partial(outer_kernel, bool(extra), tile)
    out = jax.ShapeDtypeStruct((units, width), BF)
    return on_vmem(kernel, out, 24, flag, *one, *two, *extra, flags=1)


def cut_kernel(first, second, out):
    quarter = out.shape[2]
    for layer, part in enumerate((first, second)):
        for i in range(4):
            out[layer * 4 + i] = part[:, i * quarter : (i + 1) * quarter].astype(BF)


def owned_mask(piece, devices, width):
    column = lax.broadcasted_iota(jnp.int32, (devices, width), 1)
    start = lax.broadcasted_iota(jnp.int32, (devices, width), 0) * piece
    return jnp.logical_and(column >= start, column < start + piece)


def exact(left, chosen):
    high = left.astype(BF)
    rest = left - high.astype(F32)
    middle = rest.astype(BF)
    low = (rest - middle.astype(F32)).astype(BF)
    return sum(product(part, chosen, 1, 0) for part in (low, middle, high))


def unpack_kernel(piece, phase, table, out):
    devices, width = table.shape[0] // 2, phase.shape[1]
    mask = owned_mask(piece, devices, width)
    lane = lax.broadcasted_iota(jnp.int32, (LANES, width), 0)
    for vector in range(out.shape[0]):
        spread = exact(table[...], (lane - vector * piece == phase[...]).astype(BF))
        for layer in range(2):
            rows = spread[layer * devices : (layer + 1) * devices]
            out[vector, layer : layer + 1] = jnp.sum(jnp.where(mask, rows, 0.0), axis=0, keepdims=True)


def pack_kernel(piece, phase, grads, out):
    devices, width = out.shape[1], phase.shape[0]
    mask = owned_mask(piece, devices, width)
    lane = lax.broadcasted_iota(jnp.int32, (width, LANES), 1)
    for layer in range(2):
        total = jnp.zeros((devices, LANES), F32)
        for vector in range(grads.shape[0]):
            rows = jnp.broadcast_to(grads[vector, layer : layer + 1], (devices, width))
            total += exact(jnp.where(mask, rows, 0.0), (lane - vector * piece == phase[...]).astype(BF))
        out[layer] = total


def unpack_vectors(table, width):
    piece = width // 64
    phase = (jnp.arange(width, dtype=jnp.int32) % piece)[None]
    out = jax.ShapeDtypeStruct((6, 2, width), F32)
    return on_vmem(functools.partial(unpack_kernel, piece), out, 16, phase, table)


def pack_vectors(grads):
    width = grads.shape[2]
    piece = width // 64
    phase = (jnp.arange(width, dtype=jnp.int32) % piece)[:, None]
    out = jax.ShapeDtypeStruct((2, 64, LANES), F32)
    return on_vmem(functools.partial(pack_kernel, piece), out, 16, phase, grads)


def tie(*values):
    return lax.optimization_barrier(values)


def ring(value, axis, step):
    return lax.ppermute(value, axis, [(i, (i + step) % 4) for i in range(4)])


def spread_near(rows):
    return ring(rows, "z", 1), ring(rows, "z", -1)


def spread_far(near):
    below, above = near
    half = below.shape[0] // 2
    return ring(below[:half], "z", 1), ring(above[half:], "z", -1)


def join(rows, near, far):
    return jnp.concatenate([rows, *near, *far], axis=0)


def chunks_of(summand):
    count = summand.shape[0] // 4
    low = summand.astype(BF)
    return [low[i * count : (i + 1) * count] for i in range(4)]


def collect_far(chunks, axis="z"):
    far = chunks[3]
    half = far.shape[0] // 2
    return ring(far[:half], axis, 1), ring(far[half:], axis, -1)


def collect_near(chunks, passed, axis="z"):
    own, below, above, _ = chunks
    half = own.shape[0] // 2
    above_one = (above[:half].astype(F32) + passed[0].astype(F32)).astype(BF)
    below_two = (below[half:].astype(F32) + passed[1].astype(F32)).astype(BF)
    from_below = ring(jnp.concatenate([above_one, above[half:]], axis=0), axis, 1)
    from_above = ring(jnp.concatenate([below[:half], below_two], axis=0), axis, -1)
    return own.astype(F32) + from_below.astype(F32) + from_above.astype(F32)


def pad_heads(rows, hd):
    return jnp.pad(rows, ((0, 0), (0, LANES - hd), (0, 0))).reshape(4 * LANES, rows.shape[2])


def attn_weights(own, other, on_first):
    first, second = pick(on_first, own, other), pick(on_first, other, own)
    hd = own.shape[1] // 2
    w_query = pad_heads(first[:, :hd], hd)
    w_pair = jnp.concatenate([pad_heads(first[:, hd:], hd), pad_heads(second[:, :hd], hd)])
    return w_query, w_pair, pad_heads(second[:, hd:], hd)


def mlp_weights(own, other, on_first):
    shape = (-1, own.shape[2])
    return pick(on_first, own, other).reshape(shape), pick(on_first, other, own).reshape(shape)


def from_owners(part):
    rows, quarter = part.shape[1:]
    sent = jnp.broadcast_to(part[None], (4, 2, rows, quarter)).reshape(8, rows, quarter)
    arrived = lax.all_to_all(sent, ("xl", "xh", "c"), 0, 0).reshape(2, 4, rows, quarter)
    return [jnp.concatenate([arrived[layer, i] for i in range(4)], axis=-1) for layer in range(2)]


def to_owners(parts):
    rows, width = parts[0].shape
    out = jax.ShapeDtypeStruct((8, rows, width // 4), BF)
    chunks = on_vmem(cut_kernel, out, 16, *parts)
    arrived = lax.all_to_all(chunks, ("xl", "xh", "c"), 0, 0)
    return jnp.sum(arrived.reshape(4, 2, rows, width // 4).astype(F32), axis=0)


def by_xor(values, index):
    odd, high = index % 2 == 1, index >= 2
    values = [pick(odd, values[i ^ 1], values[i]) for i in range(4)]
    return [pick(high, values[i ^ 2], values[i]) for i in range(4)]


def token_routes():
    routes = []
    for step in range(4):
        route = []
        for a in range(2):
            for b in range(2):
                for y in range(4):
                    m = (2 * a + y % 2) ^ step
                    route.append(((a * 2 + b) * 4 + y, (b * 2 + y // 2) * 4 + m))
        routes.append(route)
    return routes


def x_ring():
    order = [xl_at * 2 + xh_at for xh_at in range(2) for xl_at in range(2)]
    up = [(order[i], order[(i + 1) % 4]) for i in range(4)]
    return up, [(b, a) for a, b in up]


def from_owners_ring(part, on_first):
    kept, given = pick(on_first, part[0], part[1]), pick(on_first, part[1], part[0])
    got = swap(given, "c")
    block = jnp.concatenate([pick(on_first, kept, got), pick(on_first, got, kept)], axis=-1)
    half = block.shape[0] // 2
    up, down = x_ring()
    below, above = lax.ppermute(block, ("xl", "xh"), up), lax.ppermute(block, ("xl", "xh"), down)
    far = jnp.concatenate(
        [lax.ppermute(below[:half], ("xl", "xh"), up), lax.ppermute(above[half:], ("xl", "xh"), down)]
    )
    turn = 2 * lax.axis_index("xh") + lax.axis_index("xl")

    def source(x):
        away = (x - turn) % 4
        return pick(away == 0, block, pick(away == 1, above, pick(away == 2, far, below)))

    return [jnp.concatenate([source(layer), source(layer + 2)], axis=-1) for layer in range(2)]


def forward_layer(hidden, rows1, attn_own, mlp_own, vectors, b_query, b_pair, b_up, hd, on_first, attn_other, late, beside):
    w_query, w_pair, w_out = attn_weights(attn_own, attn_other, on_first)
    own = (dot("nd,fd->nf", rows1, w_pair) + b_pair).astype(BF)
    other = swap(own, "c")
    query = (dot("nd,fd->nf", rows1, w_query) + b_query).astype(BF)
    attn = attend(query, own, other, hd)
    attn, beside = tie(attn, beside)
    chunks = chunks_of(dot("nf,fd->nd", attn, w_out))
    passed, mlp_own = tie(collect_far(chunks), mlp_own)
    branch, mlp_other = tie(collect_near(chunks, passed), swap(mlp_own, "c"))
    middle = hidden + (branch + vectors[3])
    a2, unit2, rstd2 = norm_rows(middle, vectors[1], vectors[4])
    near, (w_up, w_down) = tie(spread_near(a2), mlp_weights(mlp_own, mlp_other, on_first))
    rows2 = join(a2, near, spread_far(near))
    pre = dot("nd,kd->nk", rows2, w_up) + b_up
    act = gelu_tanh(pre).astype(BF)
    stored = (rows1, query, own, other, attn, unit2, rstd2, rows2, pre, act)
    weights = (w_query, w_pair, w_out, w_up, w_down)
    if late is None:
        return middle, stored, weights, beside
    chunks = chunks_of(dot("nk,kd->nd", act, w_down))
    summed, held = tie(collect_near(chunks, collect_far(chunks)), late(mlp_own))
    result = middle + (summed + vectors[5])
    return result, stored, weights, held, beside


def backward_layer(grad_out, down_rows, stored, unit_rows, unit1, rstd1, weights, vectors, on_first, hd, beside, to_owner):
    rows1, query, own, other, attn, unit2, rstd2, rows2, pre, act = stored
    w_query, w_pair, w_out, w_up, w_down = weights
    grad_act = dot("nd,kd->nk", down_rows, w_down)
    grad_pre = jax.vjp(gelu_tanh, pre)[1](grad_act)[0]
    pre_low = grad_pre.astype(BF)
    summand = dot("nk,kd->nd", pre_low, w_up).astype(BF)
    if beside is not None:
        beside = chunks_of(dot("nk,kd->nd", beside, w_down))
        summand, pre_low, beside_passed = tie(summand, pre_low, collect_far(beside))
    else:
        summand, pre_low = tie(summand, pre_low)
    chunks = chunks_of(summand)
    up_pair, down_pair = (pre_low, rows2), (act, down_rows)
    flag = on_first.astype(jnp.int32).reshape(1)
    ga2, given = tie(collect_near(chunks, collect_far(chunks)), outer(flag, down_pair, up_pair))
    grad_middle, gain2, offset2 = norm_back(grad_out, ga2, unit2, rstd2, vectors[1])
    go = grad_middle.astype(BF)
    near, part_mlp = tie(spread_near(go), outer(flag, up_pair, down_pair, swap(given, "c")))
    part_mlp = lax.psum_scatter(part_mlp.reshape(4, -1, part_mlp.shape[1]), "y", scatter_dimension=0, tiled=False)
    far = spread_far(near)
    if beside is not None:
        far, beside_passed = tie(far, beside_passed)
    out_rows = join(go, near, far)
    gattn = dot("nd,fd->nf", out_rows, w_out).astype(BF)
    grad_query, sum_query, grad_own, grad_other = attend_back(query, own, other, gattn, hd)
    if beside is not None:
        grad_other, beside = tie(grad_other, collect_near(beside, beside_passed))
    sent = swap(grad_other, "c")
    grad_w_out = dot("nf,nd->fd", attn, out_rows).astype(BF)
    grad_w_query = dot("nf,nd->fd", grad_query, rows1).astype(BF)
    from_query = dot("nf,fd->nd", grad_query, w_query)
    sent, part_mlp, grad_w_out, grad_w_query, from_query = tie(sent, part_mlp, grad_w_out, grad_w_query, from_query)
    part_mlp = to_owner(part_mlp)
    pair = grad_own + sent.astype(F32)
    sum_value = jnp.sum(pair[1], axis=0)
    pair = pair.astype(BF)
    partial = from_query + dot("nf,fd->nd", jnp.concatenate([pair[0], pair[1]], axis=1), w_pair)
    gain1, offset1 = jnp.sum(partial * unit_rows, axis=0), jnp.sum(partial, axis=0)
    chunks = chunks_of(partial)

    def heads(rows):
        return rows.reshape(4, LANES, -1)[:, :hd]

    def attn_grads(pair):
        grad_w_key, grad_w_value = (dot("nf,nd->fd", pair[i], rows1).astype(BF) for i in range(2))
        first = jnp.concatenate([heads(grad_w_query), heads(grad_w_key)], axis=1)
        second = jnp.concatenate([heads(grad_w_value), heads(grad_w_out)], axis=1)
        return pick(on_first, second, first), pick(on_first, first, second)

    passed, pair = tie(collect_far(chunks), pair)
    given, kept = attn_grads(pair)
    part_attn = (kept.astype(F32) + swap(given, "c").astype(F32)).astype(BF)
    ga1, gain1, offset1, part_mlp = tie(collect_near(chunks, passed), gain1, offset1, part_mlp)
    grad_hidden = norm_back(grad_middle, ga1, unit1, rstd1, vectors[0])[0]
    grad_vectors = [gain1, gain2, offset1, jnp.sum(grad_middle, axis=0), offset2, jnp.sum(grad_out, axis=0)]
    grad_b_up = jnp.sum(grad_pre, axis=0)
    grad_b_qv = jnp.stack([sum_query[0], sum_value]).reshape(2, 4, LANES)
    return grad_hidden, part_attn, part_mlp, (grad_vectors, grad_b_qv, grad_b_up), beside


def body(ends_in, w_qkv, b_qv, w_out, w_up, b_up, w_down, gains, shifts):
    xl, core, own_y, own_z = (lax.axis_index(axis) for axis in ("xl", "c", "y", "z"))
    local = ends_in[0, :, 0]
    _, rows, width = local.shape
    hd = w_qkv.shape[3]
    units = w_up.shape[2]
    padded = -(-units // 16) * 16
    spare = padded - units

    on_first = core == 0
    qkv_rows = jnp.transpose(w_qkv[0], (1, 2, 0))
    pad_rows = ((0, spare), (0, 0))
    attn_rows = jnp.stack([qkv_rows[:2].reshape(2 * hd, -1), jnp.concatenate([qkv_rows[2], w_out[0]], axis=0)])
    mlp_rows = jnp.stack([jnp.pad(w_up[0].T, pad_rows), jnp.pad(w_down[0], pad_rows)])
    attn_rows, local = tie(attn_rows, local)
    attn_parts = from_owners(attn_rows)

    place = 2 * xl + own_y % 2
    routes = token_routes()
    blocks = by_xor([local[m] for m in range(4)], place)
    blocks = [lax.ppermute(block, ("xl", "c", "y"), route) for block, route in zip(blocks, routes)]
    blocks = by_xor(blocks, own_y)
    start_low, cot_low = jnp.concatenate(blocks[:2]), jnp.concatenate(blocks[2:])
    piece = width // 64
    up_lines = -(-padded // LANES)
    lines = -(-(3 + up_lines) // 8) * 8

    def line(values, count):
        return jnp.pad(values, (0, count * LANES - values.shape[0])).reshape(count, LANES)

    own = [line(jnp.concatenate([gains[0].ravel(), shifts[0].ravel()]), 1), line(b_qv[0, 0], 1), line(b_qv[0, 1], 1)]
    own = jnp.concatenate(own + [line(b_up[0], lines - 3)])[None]
    near = spread_near(start_low)
    own, attn0_part, mlp_rows = tie(own, attn_parts[0], mlp_rows)
    attn0_own = lax.all_gather(attn0_part, "y", axis=0)
    table = lax.all_to_all(jnp.broadcast_to(own, (128, lines, LANES)), AXES, 0, 0)
    start_rows = join(start_low, near, spread_far(near))
    mlp_parts = from_owners_ring(mlp_rows, on_first)
    attn0_own, mlp_parts, attn1_part = tie(attn0_own, mlp_parts, attn_parts[1])
    mlp0_own = lax.all_gather(mlp_parts[0], "y", axis=0)
    part1 = jnp.concatenate([attn1_part, mlp_parts[1]])

    vectors = jnp.swapaxes(unpack_vectors(table[:, 0], width), 0, 1)
    biases = lax.dynamic_index_in_dim(table.reshape(2, 4, 4, 4, lines, LANES)[:, 0], own_z, 2, keepdims=False)
    bias_qv = biases[:, :, 1:3].transpose(0, 2, 1, 3)
    bias_up = biases[:, :, 3 : 3 + up_lines].reshape(2, 4, -1)[..., :padded].reshape(2, -1)
    bias_qv = bias_qv.reshape(2, 2, 4 * LANES)
    bias_pair = jnp.concatenate([jnp.zeros_like(bias_qv[:, 1]), bias_qv[:, 1]], axis=-1)

    start, cotangent = start_low.astype(F32), cot_low.astype(F32)
    rows0, unit_rows0, _ = norm_rows(start_rows.astype(F32), vectors[0, 0], vectors[0, 2])
    _, unit0, rstd0 = norm_rows(start, vectors[0, 0], vectors[0, 2])
    def fetch_next(after):
        own = tie(after, part1)[1]
        return lax.all_gather(own, "y", axis=0)

    middle, stored0, weights0, own1, cot_near = forward_layer(
        start, rows0, attn0_own, mlp0_own, vectors[0], bias_qv[0, 0], bias_pair[0], bias_up[0], hd, on_first,
        swap(attn0_own, "c"), fetch_next, spread_near(cot_low),
    )
    attn1_own, mlp1_own = own1[:, : 2 * hd], own1[:, 2 * hd :]
    middle = middle.astype(BF)
    near, attn1_own, attn1_other = tie(spread_near(middle), attn1_own, swap(attn1_own, "c"))
    middle_rows = join(middle, near, spread_far(near)).astype(F32)
    middle = middle.astype(F32)
    rows1, unit_rows1, _ = norm_rows(middle_rows, vectors[1, 0], vectors[1, 2])
    _, unit1, rstd1 = norm_rows(middle, vectors[1, 0], vectors[1, 2])
    middle1, stored1, weights1, cot_far = forward_layer(
        middle, rows1, attn1_own, mlp1_own, vectors[1], bias_qv[1, 0], bias_pair[1], bias_up[1], hd, on_first,
        attn1_other, None, spread_far(cot_near),
    )
    down_rows = join(cot_low, cot_near, cot_far)
    grad1, attn1, mlp1, small1, branch = backward_layer(
        cotangent, down_rows, stored1, unit_rows1, unit1, rstd1, weights1, vectors[1], on_first, hd,
        stored1[-1], lambda part: part,
    )
    result = middle1 + (branch + vectors[1, 5])
    grad1 = grad1.astype(BF)
    near, attn1 = tie(spread_near(grad1), attn1)
    attn1 = lax.psum_scatter(attn1, "y", scatter_dimension=0, tiled=False)
    down_rows = join(grad1, near, spread_far(near))
    grad0, attn0, grad_mlp, small0, _ = backward_layer(
        grad1.astype(F32), down_rows, stored0, unit_rows0, unit0, rstd0, weights0, vectors[0], on_first, hd, None,
        lambda part: to_owners((part, mlp1)),
    )
    gvec1, gqv1, gup1 = small1
    gvec0, gqv0, gup0 = small0

    chunks = [lax.dynamic_index_in_dim(attn0, (own_y + step) % 4, 0, keepdims=False) for step in (0, 3, 1, 2)]
    half = rows
    out_grad, out_result = grad0.astype(BF), result.astype(BF)
    blocks = by_xor([out_grad[:half], out_grad[half:], out_result[:half], out_result[half:]], own_y)
    attn0, blocks = tie(collect_near(chunks, collect_far(chunks, "y"), "y"), blocks)
    blocks = [
        lax.ppermute(block, ("xl", "c", "y"), [(b, a) for a, b in route]) for block, route in zip(blocks, routes)
    ]
    ends_out = jnp.stack(by_xor(blocks, place))

    grad_vectors = jnp.stack(gvec0 + gvec1).reshape(2, 6, width).swapaxes(0, 1)
    grad_qv = jnp.stack([gqv0, gqv1]).transpose(0, 2, 1, 3)
    grad_up = jnp.stack([gup0, gup1]).reshape(2, 4, padded)
    grad_up = jnp.pad(grad_up, ((0, 0), (0, 0), (0, (lines - 3) * LANES - padded)))
    grad_bias = jnp.concatenate([grad_qv, grad_up.reshape(2, 4, lines - 3, LANES)], axis=2)
    here = (jnp.arange(4) == own_z)[:, None, None]
    grad_bias = jnp.where(here, grad_bias[:, None, :, None], 0.0)
    grad_bias = jnp.broadcast_to(grad_bias, (2, 4, 4, 4, lines - 1, LANES)).reshape(128, lines - 1, LANES)
    sent = jnp.concatenate([pack_vectors(grad_vectors).reshape(128, 1, LANES), grad_bias], axis=1)

    grad_attn, sent = tie(to_owners((attn0, attn1)), sent)
    owned = lax.all_to_all(sent, AXES, 0, 0)
    owned = jnp.sum(owned, axis=0)
    share_vec = owned[0, : 6 * piece].reshape(6, piece)
    share_qv = owned[1:3, :hd]
    share_b_up = owned[3:].reshape(-1)[:units]
    share_up = grad_mlp[0, :units].T
    share_down = grad_mlp[1, :units]
    heads = grad_attn.reshape(4, hd, -1)
    share_qkv = jnp.transpose(heads[:3], (2, 0, 1))
    share_out = heads[3]

    return (
        ends_out[None, :, None],
        share_qkv[None],
        share_qv[None],
        share_out[None],
        share_up[None],
        share_b_up[None],
        share_down[None],
        share_vec[None, :2],
        share_vec[None, 2:],
    )


def solution(mesh):
    fine = Mesh(mesh.devices.reshape(2, 2, 2, 4, 4), AXES)
    f, t = ("xh", "c"), ("y", "z")
    specs = (
        P("xl", None, f, t, None),
        P("xl", f, None, t),
        P("xl", None, t),
        P("xl", t, f),
        P("xl", f, t),
        P("xl", t),
        P("xl", t, f),
        P("xl", None, f + t),
        P("xl", None, f + t),
    )
    return jax.shard_map(body, mesh=fine, in_specs=specs, out_specs=specs, check_vma=False)
```
